32 devices in a mesh: ens: 2 (over y), sfc: 4 (over z), lev: 2 (over x), trc: 2 (over core).
Axes of the slice: x: 2, y: 2, z: 4, core: 2. Of those that a mesh axis runs over, the one named last changes fastest.
Arguments:
- tracers: float32 [16, 16, 16, 4096], P('trc', 'lev', None, ('ens', 'sfc')), parts along dimension 3, may hold values from 0.2 to 2
- velocity: float32 [16, 2, 16, 4096], P('lev', None, None, ('ens', 'sfc')), parts along dimension 3, may hold values from -4 to 4
- node_mass: float32 [16, 2048], P(None, 'sfc'), may hold values from 0.25 to 4
- inverse_mass: float32 [16, 2048], P(None, 'sfc'), may hold values from 0.02 to 4, as said below
- edge_slots: int32 [4, 2048], P(None, 'sfc'), may hold values from 0 to 767, as said below
- send_rows: int32 [2, 512], P(None, 'sfc'), may hold values from 0 to 511, as said below
- land_water: float32 [16, 8192], P('trc', ('ens', 'sfc')), parts along dimension 1, may hold values from 0.1 to 3
- evap_factor: float32 [4096], P('sfc'), may hold values from 0.1 to 1
- land_counts: int32 [4], P('sfc'), may hold values from 256 to 1024, as said below
- land_slot: int32 [4, 4, 128], P('sfc'), may hold values from 0 to 1023, as said below
- atmos_node: int32 [4, 4, 128], P('sfc'), may hold values from 0 to 8191, as said below
- weight_to_atmos: float32 [4, 4, 128], P('sfc'), may hold values from 0 to 8, as said below
- weight_to_land: float32 [4, 4, 128], P('sfc'), may hold values from 0 to 0.4, as said below
- rain_rate: float32 [16], P('lev'), may hold values from 0.02 to 0.2
Outputs:
- tracers_out: float32 [16, 16, 16, 4096], P('trc', 'lev', None, ('ens', 'sfc')), parts along dimension 3
- land_out: float32 [16, 8192], P('trc', ('ens', 'sfc')), parts along dimension 1
The draws below stay inside these ranges and needn't reach their ends.
There are 2 independent parts, one for each index of `ens`. The reference program is written for one: setup_inputs(seed, part) draws one part's arguments, and reference() takes and returns one part's arrays. A program takes and returns all parts, laid end to end along the dimension named above; an argument that names none is the same for every part. Nothing has to cross between parts.
Inputs may be any that keep to these rules, and one draw needn't show every extreme that they name: `edge_slots`: the element grid has 128 elements a row and 4 rows a partition, partitions follow one another along the curve, and it closes in both directions. Values under 512 are local positions in the same partition; then come the positions in the lower partition's list send_rows[1] and in the upper partition's list send_rows[0]. `send_rows`: row 0 holds the local positions of the partition's lowest-row elements, row 1 those of its highest-row elements, each row in an order of its own. `land_counts`: one partition has 1024 live cells. `land_slot`: each pair has 32 to 128 live entries first, the rest are 0 with weight 0; live entries name live slots. Some atmosphere partition receives 128 live entries from every land partition, and some land partition sends 128 to every atmosphere partition. `atmos_node`: the same entries seen from the atmosphere side; unused ones are 0. `weight_to_atmos`: zero exactly on unused entries. `weight_to_land`: zero exactly on unused entries. `inverse_mass`: the reciprocal of node_mass plus node_mass at the matching nodes of the element's edge neighbours.
All inputs are finite; a program needn't handle non-finite values.
Results may differ from the reference program's by a relative error of at most 0.0001.
Values sent between devices are 32-bit elements; how exact they have to be, the bound alone decides.
A program may use at most 128 MiB of HBM per device.

```python
import math
import jax
import jax.numpy as jnp
import numpy as np
from jax import lax

TRACERS = 16
LEVELS = 16
NODES = 16
SUBSTEPS = 4
ROW_ELEMS = 128
ROWS_DEV = 4
LAND_DEV = 1024
BLOCK = 128
PARTITIONS = 4
ELEM_DEV = 512
ELEMS = 2048
LAND = 4096


def edge_table():
    return np.array([[0, 1, 2, 3], [3, 7, 11, 15], [12, 13, 14, 15], [0, 4, 8, 12]])


def grid_tables(key):
    key_list = jax.random.split(key, 3)
    position = jax.vmap(lambda subkey: jax.random.permutation(subkey, ELEM_DEV))(jax.random.split(key_list[0], PARTITIONS)).astype(jnp.int32)
    lower_order = jax.vmap(lambda subkey: jax.random.permutation(subkey, ROW_ELEMS))(jax.random.split(key_list[1], PARTITIONS)).astype(jnp.int32)
    upper_order = jax.vmap(lambda subkey: jax.random.permutation(subkey, ROW_ELEMS))(jax.random.split(key_list[2], PARTITIONS)).astype(jnp.int32)
    lower_cells = position[:, :ROW_ELEMS]
    upper_cells = position[:, (ROWS_DEV - 1) * ROW_ELEMS:]
    send_lower = jnp.take_along_axis(lower_cells, lower_order, axis=1)
    send_upper = jnp.take_along_axis(upper_cells, upper_order, axis=1)
    lower_rank = jnp.argsort(lower_order, axis=1).astype(jnp.int32)
    upper_rank = jnp.argsort(upper_order, axis=1).astype(jnp.int32)
    partition = jnp.arange(PARTITIONS, dtype=jnp.int32)
    below = (partition - 1) % PARTITIONS
    above = (partition + 1) % PARTITIONS
    cell_index = jnp.arange(ELEM_DEV, dtype=jnp.int32)
    cell_row = cell_index // ROW_ELEMS
    cell_column = cell_index % ROW_ELEMS
    east_cell = cell_row * ROW_ELEMS + (cell_column + 1) % ROW_ELEMS
    west_cell = cell_row * ROW_ELEMS + (cell_column - 1) % ROW_ELEMS
    south_cell = jnp.clip((cell_row - 1) * ROW_ELEMS + cell_column, 0, ELEM_DEV - 1)
    north_cell = jnp.clip((cell_row + 1) * ROW_ELEMS + cell_column, 0, ELEM_DEV - 1)
    has_south = (cell_row > 0)[None]
    has_north = (cell_row < ROWS_DEV - 1)[None]
    south_slot = jnp.where(has_south, position[:, south_cell], ELEM_DEV + upper_rank[below][:, cell_column])
    north_slot = jnp.where(has_north, position[:, north_cell], ELEM_DEV + ROW_ELEMS + lower_rank[above][:, cell_column])
    slots_cell = jnp.stack([south_slot, position[:, east_cell], north_slot, position[:, west_cell]])
    base = partition[:, None] * ELEM_DEV
    south_global = jnp.where(has_south, base + position[:, south_cell], below[:, None] * ELEM_DEV + position[below][:, (ROWS_DEV - 1) * ROW_ELEMS + cell_column])
    north_global = jnp.where(has_north, base + position[:, north_cell], above[:, None] * ELEM_DEV + position[above][:, cell_column])
    global_cell = jnp.stack([south_global, base + position[:, east_cell], north_global, base + position[:, west_cell]])
    cell_at = jnp.argsort(position, axis=1).astype(jnp.int32)
    slots_store = jnp.take_along_axis(slots_cell, jnp.broadcast_to(cell_at[None], slots_cell.shape), axis=2).reshape(4, ELEMS)
    global_store = jnp.take_along_axis(global_cell, jnp.broadcast_to(cell_at[None], global_cell.shape), axis=2).reshape(4, ELEMS)
    send_both = jnp.stack([send_lower, send_upper]).reshape(2, PARTITIONS * ROW_ELEMS)
    return (slots_store.astype(jnp.int32), send_both.astype(jnp.int32), global_store.astype(jnp.int32))


def mass_field(key, lowest, highest):
    edge_nodes = edge_table()
    slots_store, send_both, global_store = grid_tables(key)
    mass_key = jax.random.fold_in(key, 101)
    node_mass = jnp.exp(jax.random.uniform(mass_key, (NODES, ELEMS), jnp.float32, math.log(lowest), math.log(highest)))
    assembled = node_mass
    for edge_side in range(4):
        across = node_mass[edge_nodes[(edge_side + 2) % 4]][:, global_store[edge_side]]
        assembled = assembled.at[edge_nodes[edge_side]].add(across)
    return (node_mass, 1.0 / assembled)


def intersection_tables(key):
    key_list = jax.random.split(jax.random.fold_in(key, 202), 8)
    partition = jnp.arange(PARTITIONS, dtype=jnp.int32)
    counts = jax.random.randint(key_list[0], (PARTITIONS,), LAND_DEV // 4, LAND_DEV + 1)
    fullest = jax.random.randint(key_list[1], (), 0, PARTITIONS)
    emptiest = (fullest + 1 + jax.random.randint(key_list[2], (), 0, PARTITIONS - 1)) % PARTITIONS
    counts = jnp.where(partition == fullest, LAND_DEV, counts)
    counts = jnp.where(partition == emptiest, LAND_DEV // 4, counts).astype(jnp.int32)
    pair_sizes = jax.random.randint(key_list[3], (PARTITIONS, PARTITIONS), BLOCK // 4, BLOCK + 1)
    busy_land = jax.random.randint(key_list[4], (), 0, PARTITIONS)
    busy_atmos = jax.random.randint(key_list[5], (), 0, PARTITIONS)
    pair_sizes = jnp.where((partition[:, None] == busy_land) | (partition[None, :] == busy_atmos), BLOCK, pair_sizes)
    entry_rank = jnp.arange(BLOCK, dtype=jnp.int32)
    live_entry = entry_rank[None, None] < pair_sizes[:, :, None]
    land_pick = jax.random.randint(key_list[6], (PARTITIONS, PARTITIONS, BLOCK), 0, counts[:, None, None])
    land_pick = jnp.where((partition[None, :, None] == busy_atmos) & (entry_rank[None, None] == 0), counts[:, None, None] - 1, land_pick)
    land_slot = jnp.where(live_entry, land_pick, 0).astype(jnp.int32)
    atmos_pick = jax.random.randint(key_list[7], (PARTITIONS, PARTITIONS, BLOCK), 0, NODES * ELEM_DEV)
    atmos_pick = jnp.where((partition[None, :, None] == busy_land) & (entry_rank[None, None] == 0), NODES * ELEM_DEV - 1, atmos_pick)
    live_atmos = jnp.transpose(live_entry, (1, 0, 2))
    atmos_node = jnp.where(live_atmos, atmos_pick, 0).astype(jnp.int32)
    return (counts, land_slot, atmos_node, live_entry)


def draw_node_mass(key, part):
    return mass_field(key, 0.5, 2.0)[0]


def draw_inverse_mass(key, part):
    return mass_field(key, 0.5, 2.0)[1]


def draw_edge_slots(key, part):
    return grid_tables(key)[0]


def draw_send_rows(key, part):
    return grid_tables(key)[1]


def draw_land_counts(key, part):
    return intersection_tables(key)[0]


def draw_land_slot(key, part):
    return intersection_tables(key)[1]


def draw_atmos_node(key, part):
    return intersection_tables(key)[2]


def draw_weight_to_atmos(key, part):
    live_entry = intersection_tables(key)[3]
    key = jax.random.fold_in(key, 5)
    shape = (PARTITIONS, PARTITIONS, BLOCK)
    values = jnp.exp(jax.random.uniform(key, shape, jnp.float32, math.log(2.0), math.log(8.0)))
    return jnp.where(live_entry, values, 0.0).astype(jnp.float32)


def draw_weight_to_land(key, part):
    live_entry = jnp.transpose(intersection_tables(key)[3], (1, 0, 2))
    key = jax.random.fold_in(key, 6)
    shape = (PARTITIONS, PARTITIONS, BLOCK)
    values = jnp.exp(jax.random.uniform(key, shape, jnp.float32, math.log(0.1), math.log(0.4)))
    return jnp.where(live_entry, values, 0.0).astype(jnp.float32)


def steps_of(own_key, shape, cuts, smallest, high):
    factor_of, own = 1.0, jax.random.fold_in(own_key, 6)
    for dim, parts in cuts:
        steps = jnp.exp(jax.random.uniform(jax.random.fold_in(own, dim), (parts,), jnp.float32, smallest / len(cuts), high / len(cuts)))
        factor_of = factor_of * jnp.repeat(steps, shape[dim] // parts).reshape([-1 if axis == dim else 1 for axis in range(len(shape))])
    return factor_of


def scatter_about(stream_key, dims, scale, most, cuts=(), kind=jnp.bfloat16):
    level = steps_of(stream_key, dims, cuts, -0.22, 0.18) if cuts else 1.0
    entries = jax.random.normal(stream_key, dims, jnp.float32) * scale * level
    return jnp.minimum(jnp.maximum(entries, -most), most).astype(kind)


def setup_inputs(seed: int = 0, part: int = 0) -> dict:
    key_of = jax.random.split(jax.random.key(seed), 15)
    own_keys = jax.random.split(jax.random.fold_in(key_of[14], part), 15)
    return {
        "tracers": jnp.clip(jnp.exp(math.log(2.0) - 2.3025851 * jax.random.uniform(own_keys[0], (TRACERS, LEVELS, NODES, ELEMS), jnp.float32) ** steps_of(own_keys[0], (TRACERS, LEVELS, NODES, ELEMS), ((0, 2), (1, 2), (3, 4)), -0.2, 0.2)), 0.2, 2.0),
        "velocity": scatter_about(own_keys[1], (LEVELS, 2, NODES, ELEMS), 1.0, 4.0, ((0, 2), (3, 4)), jnp.float32),
        "node_mass": draw_node_mass(jax.random.fold_in(key_of[14], 71), part),
        "inverse_mass": draw_inverse_mass(jax.random.fold_in(key_of[14], 71), part),
        "edge_slots": draw_edge_slots(jax.random.fold_in(key_of[14], 71), part),
        "send_rows": draw_send_rows(jax.random.fold_in(key_of[14], 71), part),
        "land_water": jnp.clip(jnp.exp(math.log(3.0) - 3.4011974 * jax.random.uniform(own_keys[6], (TRACERS, LAND), jnp.float32) ** steps_of(own_keys[6], (TRACERS, LAND), ((0, 2), (1, 4)), -0.2, 0.2)), 0.1, 3.0),
        "evap_factor": jnp.clip(jnp.exp(math.log(1.0) - 2.3025851 * jax.random.uniform(key_of[7], (LAND,), jnp.float32) ** steps_of(key_of[7], (LAND,), ((0, 4),), -0.2, 0.2)), 0.1, 1.0),
        "land_counts": draw_land_counts(jax.random.fold_in(key_of[14], 71), part),
        "land_slot": draw_land_slot(jax.random.fold_in(key_of[14], 71), part),
        "atmos_node": draw_atmos_node(jax.random.fold_in(key_of[14], 71), part),
        "weight_to_atmos": draw_weight_to_atmos(jax.random.fold_in(key_of[14], 71), part),
        "weight_to_land": draw_weight_to_land(jax.random.fold_in(key_of[14], 71), part),
        "rain_rate": jnp.clip(jnp.exp(math.log(0.2) - 2.3025851 * jax.random.uniform(key_of[13], (LEVELS,), jnp.float32) ** steps_of(key_of[13], (LEVELS,), ((0, 2),), -0.2, 0.2)), 0.02, 0.2),
    }


time_step = 0.03
land_step = 0.5

def lagrange_derivative(points):
    point_count = len(points)
    matrix = np.zeros((point_count, point_count))
    for row_index in range(point_count):
        for column in range(point_count):
            if row_index != column:
                weight_row = np.prod([points[row_index] - points[other_index] for other_index in range(point_count) if other_index != row_index])
                weight_column = np.prod([points[column] - points[other_index] for other_index in range(point_count) if other_index != column])
                matrix[row_index, column] = weight_row / (weight_column * (points[row_index] - points[column]))
        matrix[row_index, row_index] = sum([1.0 / (points[row_index] - points[other_index]) for other_index in range(point_count) if other_index != row_index])
    return matrix

def gll_tables():
    gll_points = np.array([-1.0, -1.0 / math.sqrt(5.0), 1.0 / math.sqrt(5.0), 1.0])
    gll_deriv = lagrange_derivative(gll_points)
    edge_nodes = np.array([[0, 1, 2, 3], [3, 7, 11, 15], [12, 13, 14, 15], [0, 4, 8, 12]])
    deriv_east = np.kron(np.eye(4), gll_deriv)
    deriv_north = np.kron(gll_deriv, np.eye(4))
    edge_place = np.eye(16)[edge_nodes.reshape(-1)].T
    return (deriv_east, deriv_north, edge_nodes, edge_place)

def advance(tracer_field, velocity, evap_source, node_mass, inverse_mass, neighbour):
    highest = lax.Precision.HIGHEST
    deriv_east, deriv_north, edge_nodes, edge_place = gll_tables()
    east_matrix = jnp.asarray(deriv_east, jnp.float32)
    north_matrix = jnp.asarray(deriv_north, jnp.float32)
    place_matrix = jnp.asarray(edge_place, jnp.float32)
    tendency = jnp.einsum('mn,lne->lme', east_matrix, velocity[:, 0] * tracer_field, precision=highest)
    tendency = tendency + jnp.einsum('mn,lne->lme', north_matrix, velocity[:, 1] * tracer_field, precision=highest)
    advanced = tracer_field - time_step * tendency
    advanced = advanced.at[-1].add(time_step * evap_source)
    weighted = node_mass * advanced
    gathered = jnp.concatenate([jnp.take(weighted[:, edge_nodes[(edge_side + 2) % 4]], neighbour[edge_side], axis=2) for edge_side in range(4)], axis=1)
    return (weighted + jnp.einsum('nc,lce->lne', place_matrix, gathered, precision=highest)) * inverse_mass

def reference(tracers, velocity, node_mass, inverse_mass, edge_slots, send_rows, land_water, evap_factor, land_counts, land_slot, atmos_node, weight_to_atmos, weight_to_land, rain_rate):
    element = jnp.arange(ELEMS, dtype=jnp.int32)
    owner_part = element // ELEM_DEV
    lower_part = (owner_part - 1) % PARTITIONS
    upper_part = (owner_part + 1) % PARTITIONS
    send_lists = send_rows.reshape(2, PARTITIONS, ROW_ELEMS)
    local_hit = owner_part[None] * ELEM_DEV + edge_slots
    from_lower = lower_part[None] * ELEM_DEV + send_lists[1][lower_part[None], jnp.clip(edge_slots - ELEM_DEV, 0, ROW_ELEMS - 1)]
    from_upper = upper_part[None] * ELEM_DEV + send_lists[0][upper_part[None], jnp.clip(edge_slots - ELEM_DEV - ROW_ELEMS, 0, ROW_ELEMS - 1)]
    neighbour = jnp.where(edge_slots < ELEM_DEV, local_hit, jnp.where(edge_slots < ELEM_DEV + ROW_ELEMS, from_lower, from_upper)).astype(jnp.int32)
    live_slots = (jnp.arange(LAND_DEV, dtype=jnp.int32)[None] < land_counts[:, None]).astype(jnp.float32).reshape(LAND)
    partition = jnp.arange(PARTITIONS, dtype=jnp.int32)
    land_flat = (partition[:, None, None] * LAND_DEV + land_slot).astype(jnp.int32)
    atmos_flat = (atmos_node // ELEM_DEV * ELEMS + partition[:, None, None] * ELEM_DEV + atmos_node % ELEM_DEV).astype(jnp.int32)
    atmos_flat_ab = jnp.transpose(atmos_flat, (1, 0, 2))
    land_flat_ba = jnp.transpose(land_flat, (1, 0, 2))

    def one_tracer(tracer_pair):
        tracer_field, soil_water = tracer_pair
        evaporation = live_slots * evap_factor * soil_water / (1.0 + soil_water)
        source_terms = (weight_to_atmos * evaporation[land_flat]).reshape(-1)
        evap_source = jnp.zeros((NODES * ELEMS,), jnp.float32).at[atmos_flat_ab.reshape(-1)].add(source_terms).reshape(NODES, ELEMS)
        for substep in range(SUBSTEPS):
            tracer_field = advance(tracer_field, velocity, evap_source, node_mass, inverse_mass, neighbour)
        rain_total = jnp.einsum('l,lne->ne', rain_rate, tracer_field, precision=lax.Precision.HIGHEST)
        rain_terms = (weight_to_land * rain_total.reshape(-1)[atmos_flat]).reshape(-1)
        precipitation = jnp.zeros((LAND,), jnp.float32).at[land_flat_ba.reshape(-1)].add(rain_terms)
        return (tracer_field, live_slots * (soil_water + land_step * (precipitation - evaporation)))
    tracers_out, land_out = lax.map(one_tracer, (tracers, land_water))
    return (tracers_out, land_out)
```

```python
import functools
import math

import jax
import jax.numpy as jnp
import numpy as np
from jax import lax
from jax.experimental import pallas as pl
from jax.experimental.pallas import tpu as pltpu
from jax.sharding import PartitionSpec as P

SUBSTEPS = 4
CHUNKS = 4
LANES = 128
time_step = 0.03
land_step = 0.5
EDGES = ((0, 1, 2, 3), (3, 7, 11, 15), (12, 13, 14, 15), (0, 4, 8, 12))
MESH = pl.DeviceIdType.MESH
F32 = jnp.float32
BF16 = jnp.bfloat16


def derivative_matrix():
    points = [-1.0, -1.0 / math.sqrt(5.0), 1.0 / math.sqrt(5.0), 1.0]
    matrix = np.zeros((4, 4))
    for i in range(4):
        for m in range(4):
            if i != m:
                w_i = np.prod([points[i] - points[o] for o in range(4) if o != i])
                w_m = np.prod([points[m] - points[o] for o in range(4) if o != m])
                matrix[i, m] = w_i / (w_m * (points[i] - points[m]))
        matrix[i, i] = sum(1.0 / (points[i] - points[o]) for o in range(4) if o != i)
    matrix[np.abs(matrix) < 1e-12] = 0.0
    return matrix


def loop(count, body, unroll_to=4):
    if count <= unroll_to:
        for i in range(count):
            body(i)
    else:
        lax.fori_loop(0, count, lambda i, c: (body(i), c)[1], 0)


def split(x):
    high = x.astype(BF16)
    low = (x - high.astype(F32)).astype(BF16)
    return jnp.concatenate([high, low], axis=0)


def fold(y):
    half = y.shape[0] // 2
    return y[:half] + y[half:]


def dot(a, b):
    return jnp.dot(a, b, preferred_element_type=F32)


def dot_t(a, b):
    return lax.dot_general(a, b, (((1,), (1,)), ((), ())), preferred_element_type=F32)


def hot(rows, first, index):
    place = lax.broadcasted_iota(jnp.int32, (rows, index.shape[1]), 0) + first
    return jnp.where(place == index, 1.0, 0.0).astype(BF16)


def kernel(
    parts,
    levs,
    tr,
    vel,
    mass,
    inv,
    slots,
    rows_sent,
    water,
    factor,
    counts,
    land_slot,
    atmos_node,
    w_out,
    w_back,
    rate,
    out,
    land,
    TS,
    W,
    VB,
    MB,
    IB,
    MS,
    OH,
    OHR,
    SOH,
    LT,
    BT,
    HL,
    G,
    RA,
    EV,
    send,
    halo,
    out_e,
    in_e,
    out_r,
    in_r,
    halo_ss,
    halo_rs,
    e_ss,
    e_rs,
    r_ss,
    r_rs,
    t_sem,
):
    N, L, Q, E = W.shape
    LC = L // CHUNKS
    R = LC * Q
    tiles = E // LANES
    land_slots = water.shape[1]
    sfc = lax.axis_index("sfc")
    lev = lax.axis_index("lev")
    group = parts * levs
    mine = lev * parts + sfc

    def peer(d):
        other = lax.rem(mine + d, group)
        return other // parts, lax.rem(other, parts)

    barrier = pltpu.get_barrier_semaphore()

    def greet(d):
        l, p = peer(d + 1)
        pl.semaphore_signal(barrier, inc=1, device_id={"sfc": p, "lev": l}, device_id_type=MESH)

    loop(group - 1, greet, 8)

    def copy_in(j):
        return pltpu.make_async_copy(
            tr.at[:, pl.ds(j * LANES, LANES)], TS.at[j], t_sem.at[j]
        )

    def copy_out(j):
        return pltpu.make_async_copy(
            TS.at[j], out.at[:, pl.ds(j * LANES, LANES)], t_sem.at[j]
        )

    for j in range(tiles):
        copy_in(j).start()

    live = jnp.where(
        lax.broadcasted_iota(jnp.int32, (1, land_slots), 1) < counts[0], 1.0, 0.0
    ).astype(F32)
    w = water[...]
    evaporation = live * factor[...] * w / (1.0 + w)
    EV[...] = evaporation
    ev2 = split(evaporation)

    def gather_land(b):
        LT[b] = hot(land_slots, 0, land_slot[pl.ds(b, 1), :])
        out_e[b] = fold(dot(ev2, LT[b])) * w_out[pl.ds(b, 1), :]

    loop(parts, gather_land)
    pl.semaphore_wait(barrier, group - 1)

    def copy_e(src, dst, p):
        return pltpu.make_async_remote_copy(
            src_ref=out_e.at[src],
            dst_ref=in_e.at[dst],
            send_sem=e_ss.at[src],
            recv_sem=e_rs.at[dst],
            device_id={"sfc": p},
            device_id_type=MESH,
        )

    def start_e(d):
        p = lax.rem(sfc + d + 1, parts)
        copy_e(p, sfc, p).start()

    loop(parts - 1, start_e)
    in_e[sfc] = out_e[sfc]

    def build_slots(i):
        k, r = i // tiles, lax.rem(i, tiles)
        first = r * LANES
        OH[k, pl.ds(pl.multiple_of(first, LANES), LANES), :] = hot(
            LANES, first, slots[pl.ds(k, 1), :]
        )

    lax.fori_loop(0, 4 * tiles, lambda i, c: (build_slots(i), c)[1], 0)
    width = rows_sent.shape[1]
    OHR[0] = hot(width, E, slots[0:1, :])
    OHR[1] = hot(width, E + width, slots[2:3, :])
    SOH[0] = hot(E, 0, rows_sent[0:1, :])
    SOH[1] = hot(E, 0, rows_sent[1:2, :])

    def build_node(b):
        node = atmos_node[pl.ds(b, 1), :]
        BT[b] = hot(E, 0, lax.rem(node, E))

    loop(parts, build_node)
    for n in range(N):
        MB[n] = jnp.broadcast_to(mass[n : n + 1, :], (Q, E))
        IB[n] = jnp.broadcast_to(inv[n : n + 1, :], (Q, E))

    def turn(i, c):
        l, j = i // tiles, lax.rem(i, tiles)
        lane = pl.ds(pl.multiple_of(j * LANES, LANES), LANES)
        for n in range(N):
            W[n, l, :, lane] = TS[j, pl.ds(l * N + n, Q, stride=L * N), :]
        for d in range(2):
            v = vel[pl.ds(pl.multiple_of((l * 2 + d) * N, N), N), lane] * time_step
            for n in range(N):
                VB[d, n, l, :, lane] = jnp.broadcast_to(v[n : n + 1], (Q, LANES))
        return c

    for j in range(tiles):
        copy_in(j).wait()
    lax.fori_loop(0, L * tiles, turn, 0)

    D = derivative_matrix()

    def advect(first):
        def one(i, c):
            l, j = first + i // tiles, lax.rem(i, tiles)
            lane = pl.ds(pl.multiple_of(j * LANES, LANES), LANES)
            t = [W[n, l, :, lane] for n in range(N)]
            f = [VB[0, n, l, :, lane] * t[n] for n in range(N)]
            acc = []
            for n in range(N):
                row, i_ = n // 4, n % 4
                terms = [float(D[i_, m]) * f[4 * row + m] for m in range(4) if D[i_, m] != 0.0]
                acc.append(functools.reduce(lambda a, b: a + b, terms))
            f = [VB[1, n, l, :, lane] * t[n] for n in range(N)]
            for n in range(N):
                row, i_ = n // 4, n % 4
                terms = [float(D[row, m]) * f[4 * m + i_] for m in range(4) if D[row, m] != 0.0]
                total = functools.reduce(lambda a, b: a + b, terms)
                W[n, l, :, lane] = MB[n, :, lane] * (t[n] - (acc[n] + total))
            return c

        lax.fori_loop(0, LC * tiles, one, 0)

    def halo_copy(s, c, d):
        other = lax.rem(sfc + (parts - 1 if d == 0 else 1), parts)
        return pltpu.make_async_remote_copy(
            src_ref=send.at[s, c, d],
            dst_ref=halo.at[s, c, d],
            send_sem=halo_ss.at[s, c, d],
            recv_sem=halo_rs.at[s, c, d],
            device_id={"sfc": other},
            device_id_type=MESH,
        )

    def emit(s, c):
        @pl.when(c == CHUNKS - 1)
        def _():
            for n in range(N):
                W[n, L - 1] = W[n, L - 1] + MS[n]

        for k in range(4):
            x = jnp.concatenate(
                [W[n, pl.ds(c * LC, LC)].reshape(R, E) for n in EDGES[k]], axis=0
            )
            HL[c, k] = split(x)
        for d in range(2):
            send[s, c, d] = fold(dot(HL[c, 2 * d], SOH[d]))
            halo_copy(s, c, d).start()

    def assemble(s, c):
        for k in range(4):
            G[k] = fold(dot(HL[c, (k + 2) % 4], OH[k]))
        for d in range(2):
            halo_copy(s, c, 1 - d).wait_recv()
            G[2 * d] = G[2 * d] + fold(dot(split(halo[s, c, 1 - d]), OHR[d]))
        for n in range(N):
            x = W[n, pl.ds(c * LC, LC)]
            for k in range(4):
                for t in range(4):
                    if EDGES[k][t] == n:
                        x = x + G[k, t * R : (t + 1) * R].reshape(LC, Q, E)
            W[n, pl.ds(c * LC, LC)] = x * IB[n][None]

    lax.fori_loop(0, CHUNKS, lambda c, x: (advect(c * LC), x)[1], 0)

    def wait_e(d):
        p = lax.rem(sfc + d + 1, parts)
        copy_e(p, p, p).wait_recv()

    loop(parts - 1, wait_e)
    MS[...] = jnp.zeros_like(MS)

    def scatter_node(a):
        where = atmos_node[pl.ds(a, 1), :] // E
        x = in_e[a]
        x = jnp.concatenate([jnp.where(where == n, x, 0.0) for n in range(N)], axis=0)
        MS[...] = MS[...] + fold(dot_t(split(x), BT[a])).reshape(N, Q, E)

    loop(parts, scatter_node)
    bottom = jnp.where(lev == levs - 1, time_step, 0.0).astype(F32)
    MS[...] = MS[...] * MB[...] * bottom
    lax.fori_loop(0, CHUNKS, lambda c, x: (emit(0, c), x)[1], 0)

    def step(i, x):
        s, c = i // CHUNKS, lax.rem(i, CHUNKS)
        assemble(s, c)
        advect(c * LC)
        emit(s + 1, c)
        return x

    lax.fori_loop(0, (SUBSTEPS - 1) * CHUNKS, step, 0)
    lax.fori_loop(0, CHUNKS, lambda c, x: (assemble(SUBSTEPS - 1, c), x)[1], 0)

    def fall(n, c):
        total = rate[0] * W[n, 0]
        for l in range(1, L):
            total = total + rate[l] * W[n, l]
        RA[n] = total
        return c

    lax.fori_loop(0, N, fall, 0)
    ra2 = split(RA[...].reshape(N * Q, E))

    def gather_node(a):
        where = atmos_node[pl.ds(a, 1), :] // E
        g = fold(dot(ra2, BT[a]))
        total = jnp.where(where == 0, g[:Q], 0.0)
        for n in range(1, N):
            total = total + jnp.where(where == n, g[n * Q : (n + 1) * Q], 0.0)
        out_r[a] = total * w_back[pl.ds(a, 1), :]

    loop(parts, gather_node)

    def copy_r(d, l, p, from_l, from_p):
        return pltpu.make_async_remote_copy(
            src_ref=out_r.at[p],
            dst_ref=in_r.at[from_l, from_p],
            send_sem=r_ss.at[d],
            recv_sem=r_rs.at[from_l, from_p],
            device_id={"sfc": p, "lev": l},
            device_id_type=MESH,
        )

    def start_r(d):
        l, p = peer(d + 1)
        copy_r(d, l, p, lev, sfc).start()

    loop(group - 1, start_r, 8)
    in_r[lev, sfc] = out_r[sfc]

    def put(i, c):
        l, j = i // tiles, lax.rem(i, tiles)
        lane = pl.ds(pl.multiple_of(j * LANES, LANES), LANES)
        for n in range(N):
            TS[j, pl.ds(l * N + n, Q, stride=L * N), :] = W[n, l, :, lane]
        return c

    lax.fori_loop(0, L * tiles, put, 0)
    for j in range(tiles):
        copy_out(j).start()

    def wait_r(d):
        l, p = peer(d + 1)
        copy_r(d, l, p, l, p).wait_recv()

    loop(group - 1, wait_r, 8)
    land[...] = jnp.zeros_like(land)

    def scatter_land(b):
        x = in_r[0, b]
        for l in range(1, levs):
            x = x + in_r[l, b]
        land[...] = land[...] + fold(dot_t(split(x), LT[b]))

    loop(parts, scatter_land)
    land[...] = live * (water[...] + land_step * (land[...] - EV[...]))

    for j in range(tiles):
        copy_out(j).wait()

    def done_e(d):
        p = lax.rem(sfc + d + 1, parts)
        copy_e(p, p, p).wait_send()

    loop(parts - 1, done_e)

    def done_r(d):
        l, p = peer(d + 1)
        copy_r(d, l, p, l, p).wait_send()

    loop(group - 1, done_r, 8)

    def done_halo(i, x):
        for d in range(2):
            halo_copy(i // CHUNKS, lax.rem(i, CHUNKS), d).wait_send()
        return x

    lax.fori_loop(0, SUBSTEPS * CHUNKS, done_halo, 0)


def shards(
    tracers,
    velocity,
    node_mass,
    inverse_mass,
    edge_slots,
    send_rows,
    land_water,
    evap_factor,
    land_counts,
    land_slot,
    atmos_node,
    weight_to_atmos,
    weight_to_land,
    rain_rate,
):
    Q, L, N, E = tracers.shape
    parts = lax.axis_size("sfc")
    levs = lax.axis_size("lev")
    width = send_rows.shape[1]
    land_slots = land_water.shape[1]
    block = land_slot.shape[2]
    R = L // CHUNKS * Q
    vmem = pl.BlockSpec(memory_space=pltpu.VMEM)
    smem = pl.BlockSpec(memory_space=pltpu.SMEM)
    specs = [vmem] * 14
    specs[0] = pl.BlockSpec(memory_space=pl.ANY)
    specs[8] = smem
    specs[13] = smem
    dma = pltpu.SemaphoreType.DMA
    tracers_out, land_out = pl.pallas_call(
        functools.partial(kernel, parts, levs),
        out_shape=(
            jax.ShapeDtypeStruct((Q * L * N, E), F32),
            jax.ShapeDtypeStruct((Q, land_slots), F32),
        ),
        in_specs=specs,
        out_specs=(pl.BlockSpec(memory_space=pl.ANY), vmem),
        scratch_shapes=[
            pltpu.VMEM((E // LANES, Q * L * N, LANES), F32),
            pltpu.VMEM((N, L, Q, E), F32),
            pltpu.VMEM((2, N, L, Q, E), F32),
            pltpu.VMEM((N, Q, E), F32),
            pltpu.VMEM((N, Q, E), F32),
            pltpu.VMEM((N, Q, E), F32),
            pltpu.VMEM((4, E, E), BF16),
            pltpu.VMEM((2, width, E), BF16),
            pltpu.VMEM((2, E, width), BF16),
            pltpu.VMEM((parts, land_slots, block), BF16),
            pltpu.VMEM((parts, E, block), BF16),
            pltpu.VMEM((CHUNKS, 4, 8 * R, E), BF16),
            pltpu.VMEM((4, 4 * R, E), F32),
            pltpu.VMEM((N, Q, E), F32),
            pltpu.VMEM((Q, land_slots), F32),
            pltpu.VMEM((SUBSTEPS, CHUNKS, 2, 4 * R, width), F32),
            pltpu.VMEM((SUBSTEPS, CHUNKS, 2, 4 * R, width), F32),
            pltpu.VMEM((parts, Q, block), F32),
            pltpu.VMEM((parts, Q, block), F32),
            pltpu.VMEM((parts, Q, block), F32),
            pltpu.VMEM((levs, parts, Q, block), F32),
            dma((SUBSTEPS, CHUNKS, 2)),
            dma((SUBSTEPS, CHUNKS, 2)),
            dma((parts,)),
            dma((parts,)),
            dma((parts * levs,)),
            dma((levs, parts)),
            dma((E // LANES,)),
        ],
        compiler_params=pltpu.CompilerParams(
            collective_id=0, has_side_effects=True, vmem_limit_bytes=56 * 1024 * 1024
        ),
    )(
        tracers.reshape(Q * L * N, E),
        velocity.reshape(-1, E),
        node_mass,
        inverse_mass,
        edge_slots,
        send_rows,
        land_water,
        evap_factor.reshape(1, -1),
        land_counts,
        land_slot[0],
        atmos_node[0],
        weight_to_atmos[0],
        weight_to_land[0],
        rain_rate,
    )
    return tracers_out.reshape(Q, L, N, E), land_out


def solution(mesh):
    return jax.shard_map(
        shards,
        mesh=mesh,
        in_specs=(
            P("trc", "lev", None, ("ens", "sfc")),
            P("lev", None, None, ("ens", "sfc")),
            P(None, "sfc"),
            P(None, "sfc"),
            P(None, "sfc"),
            P(None, "sfc"),
            P("trc", ("ens", "sfc")),
            P("sfc"),
            P("sfc"),
            P("sfc", None, None),
            P("sfc", None, None),
            P("sfc", None, None),
            P("sfc", None, None),
            P("lev"),
        ),
        out_specs=(P("trc", "lev", None, ("ens", "sfc")), P("trc", ("ens", "sfc"))),
        check_vma=False,
    )
```

```python
import functools
import math

import jax
import jax.numpy as jnp
import numpy as np
from jax import lax
from jax.experimental import pallas as pl
from jax.experimental.pallas import tpu as pltpu
from jax.sharding import PartitionSpec as P

SUBSTEPS = 4
CHUNKS = 4
LANES = 128
time_step = 0.03
land_step = 0.5
EDGES = ((0, 1, 2, 3), (3, 7, 11, 15), (12, 13, 14, 15), (0, 4, 8, 12))
MESH = pl.DeviceIdType.MESH
F32 = jnp.float32
BF16 = jnp.bfloat16


def derivative_matrix():
    points = [-1.0, -1.0 / math.sqrt(5.0), 1.0 / math.sqrt(5.0), 1.0]
    matrix = np.zeros((4, 4))
    for i in range(4):
        for m in range(4):
            if i != m:
                w_i = np.prod([points[i] - points[o] for o in range(4) if o != i])
                w_m = np.prod([points[m] - points[o] for o in range(4) if o != m])
                matrix[i, m] = w_i / (w_m * (points[i] - points[m]))
        matrix[i, i] = sum(1.0 / (points[i] - points[o]) for o in range(4) if o != i)
    matrix[np.abs(matrix) < 1e-12] = 0.0
    return matrix


def loop(count, body, unroll_to=4):
    if count <= unroll_to:
        for i in range(count):
            body(i)
    else:
        lax.fori_loop(0, count, lambda i, c: (body(i), c)[1], 0)


def split(x):
    high = x.astype(BF16)
    low = (x - high.astype(F32)).astype(BF16)
    return jnp.concatenate([high, low], axis=0)


def fold(y):
    half = y.shape[0] // 2
    return y[:half] + y[half:]


def dot(a, b):
    return jnp.dot(a, b, preferred_element_type=F32)


def dot_t(a, b):
    return lax.dot_general(a, b, (((1,), (1,)), ((), ())), preferred_element_type=F32)


def hot(rows, first, index):
    place = lax.broadcasted_iota(jnp.int32, (rows, index.shape[1]), 0) + first
    return jnp.where(place == index, 1.0, 0.0).astype(BF16)


def kernel(
    parts,
    levs,
    tr,
    vel,
    mass,
    inv,
    slots,
    rows_sent,
    water,
    factor,
    counts,
    land_slot,
    atmos_node,
    w_out,
    w_back,
    rate,
    out,
    land,
    TS,
    W,
    VB,
    MB,
    IB,
    MS,
    OH,
    OHR,
    SOH,
    LT,
    BT,
    HL,
    G,
    RA,
    EV,
    send,
    halo,
    out_e,
    in_e,
    out_r,
    in_r,
    halo_ss,
    halo_rs,
    e_ss,
    e_rs,
    r_ss,
    r_rs,
    t_sem,
):
    N, L, Q, E = W.shape
    LC = L // CHUNKS
    R = LC * Q
    tiles = E // LANES
    land_slots = water.shape[1]
    sfc = lax.axis_index("sfc")
    lev = lax.axis_index("lev")
    group = parts * levs
    mine = lev * parts + sfc

    def peer(d):
        other = lax.rem(mine + d, group)
        return other // parts, lax.rem(other, parts)

    barrier = pltpu.get_barrier_semaphore()

    def greet(d):
        l, p = peer(d + 1)
        pl.semaphore_signal(barrier, inc=1, device_id={"sfc": p, "lev": l}, device_id_type=MESH)

    loop(group - 1, greet, 8)

    def copy_in(j):
        return pltpu.make_async_copy(
            tr.at[:, pl.ds(j * LANES, LANES)], TS.at[j], t_sem.at[j]
        )

    def copy_out(j):
        return pltpu.make_async_copy(
            TS.at[j], out.at[:, pl.ds(j * LANES, LANES)], t_sem.at[j]
        )

    for j in range(tiles):
        copy_in(j).start()

    live = jnp.where(
        lax.broadcasted_iota(jnp.int32, (1, land_slots), 1) < counts[0], 1.0, 0.0
    ).astype(F32)
    w = water[...]
    evaporation = live * factor[...] * w / (1.0 + w)
    EV[...] = evaporation
    ev2 = split(evaporation)

    def gather_land(b):
        LT[b] = hot(land_slots, 0, land_slot[pl.ds(b, 1), :])
        out_e[b] = fold(dot(ev2, LT[b])) * w_out[pl.ds(b, 1), :]

    loop(parts, gather_land)

    def copy_e(src, dst, p):
        return pltpu.make_async_remote_copy(
            src_ref=out_e.at[src],
            dst_ref=in_e.at[dst],
            send_sem=e_ss.at[src],
            recv_sem=e_rs.at[dst],
            device_id={"sfc": p},
            device_id_type=MESH,
        )

    SOH[0] = hot(E, 0, rows_sent[0:1, :])
    SOH[1] = hot(E, 0, rows_sent[1:2, :])
    for n in range(N):
        MB[n] = jnp.broadcast_to(mass[n : n + 1, :], (Q, E))

    def turn(i, c):
        l, j = i // tiles, lax.rem(i, tiles)
        lane = pl.ds(pl.multiple_of(j * LANES, LANES), LANES)
        for n in range(N):
            W[n, l, :, lane] = TS[j, pl.ds(l * N + n, Q, stride=L * N), :]
        for d in range(2):
            v = vel[pl.ds(pl.multiple_of((l * 2 + d) * N, N), N), lane] * time_step
            for n in range(N):
                VB[d, n, l, :, lane] = jnp.broadcast_to(v[n : n + 1], (Q, LANES))
        return c

    for j in range(tiles):
        copy_in(j).wait()
    lax.fori_loop(0, L * tiles, turn, 0)

    D = derivative_matrix()

    def advect(first):
        def one(i, c):
            l, j = first + i // tiles, lax.rem(i, tiles)
            lane = pl.ds(pl.multiple_of(j * LANES, LANES), LANES)
            t = [W[n, l, :, lane] for n in range(N)]
            f = [VB[0, n, l, :, lane] * t[n] for n in range(N)]
            acc = []
            for n in range(N):
                row, i_ = n // 4, n % 4
                terms = [float(D[i_, m]) * f[4 * row + m] for m in range(4) if D[i_, m] != 0.0]
                acc.append(functools.reduce(lambda a, b: a + b, terms))
            f = [VB[1, n, l, :, lane] * t[n] for n in range(N)]
            for n in range(N):
                row, i_ = n // 4, n % 4
                terms = [float(D[row, m]) * f[4 * m + i_] for m in range(4) if D[row, m] != 0.0]
                total = functools.reduce(lambda a, b: a + b, terms)
                W[n, l, :, lane] = MB[n, :, lane] * (t[n] - (acc[n] + total))
            return c

        lax.fori_loop(0, LC * tiles, one, 0)

    def halo_copy(s, c, d):
        other = lax.rem(sfc + (parts - 1 if d == 0 else 1), parts)
        return pltpu.make_async_remote_copy(
            src_ref=send.at[s, c, d],
            dst_ref=halo.at[s, c, d],
            send_sem=halo_ss.at[s, c, d],
            recv_sem=halo_rs.at[s, c, d],
            device_id={"sfc": other},
            device_id_type=MESH,
        )

    def emit(s, c):
        @pl.when(c == CHUNKS - 1)
        def _():
            for n in range(N):
                W[n, L - 1] = W[n, L - 1] + MS[n]

        def edge(k):
            x = jnp.concatenate(
                [W[n, pl.ds(c * LC, LC)].reshape(R, E) for n in EDGES[k]], axis=0
            )
            HL[c, k] = split(x)

        for d in range(2):
            edge(2 * d)
            send[s, c, d] = fold(dot(HL[c, 2 * d], SOH[d]))
            halo_copy(s, c, d).start()
        edge(1)
        edge(3)

    def assemble(s, c):
        for k in range(4):
            G[k] = fold(dot(HL[c, (k + 2) % 4], OH[k]))
        for d in range(2):
            halo_copy(s, c, 1 - d).wait_recv()
            G[2 * d] = G[2 * d] + fold(dot(split(halo[s, c, 1 - d]), OHR[d]))
        for n in range(N):
            x = W[n, pl.ds(c * LC, LC)]
            for k in range(4):
                for t in range(4):
                    if EDGES[k][t] == n:
                        x = x + G[k, t * R : (t + 1) * R].reshape(LC, Q, E)
            W[n, pl.ds(c * LC, LC)] = x * IB[n][None]

    pl.semaphore_wait(barrier, group - 1)
    def start_e(d):
        p = lax.rem(sfc + d + 1, parts)
        copy_e(p, sfc, p).start()

    loop(parts - 1, start_e)
    in_e[sfc] = out_e[sfc]

    def first(c, x):
        advect(c * LC)
        emit(0, c)
        return x

    lax.fori_loop(0, CHUNKS - 1, first, 0)
    def build_slots(i):
        k, r = i // tiles, lax.rem(i, tiles)
        first = r * LANES
        OH[k, pl.ds(pl.multiple_of(first, LANES), LANES), :] = hot(
            LANES, first, slots[pl.ds(k, 1), :]
        )

    lax.fori_loop(0, 4 * tiles, lambda i, c: (build_slots(i), c)[1], 0)
    width = rows_sent.shape[1]
    OHR[0] = hot(width, E, slots[0:1, :])
    OHR[1] = hot(width, E + width, slots[2:3, :])

    def build_node(b):
        node = atmos_node[pl.ds(b, 1), :]
        BT[b] = hot(E, 0, lax.rem(node, E))

    loop(parts, build_node)
    for n in range(N):
        IB[n] = jnp.broadcast_to(inv[n : n + 1, :], (Q, E))
    advect((CHUNKS - 1) * LC)

    def wait_e(d):
        p = lax.rem(sfc + d + 1, parts)
        copy_e(p, p, p).wait_recv()

    loop(parts - 1, wait_e)
    MS[...] = jnp.zeros_like(MS)

    def scatter_node(a):
        where = atmos_node[pl.ds(a, 1), :] // E
        x = in_e[a]
        x = jnp.concatenate([jnp.where(where == n, x, 0.0) for n in range(N)], axis=0)
        MS[...] = MS[...] + fold(dot_t(split(x), BT[a])).reshape(N, Q, E)

    loop(parts, scatter_node)
    bottom = jnp.where(lev == levs - 1, time_step, 0.0).astype(F32)
    MS[...] = MS[...] * MB[...] * bottom
    emit(0, CHUNKS - 1)

    def step(i, x):
        s, c = i // CHUNKS, lax.rem(i, CHUNKS)
        assemble(s, c)
        advect(c * LC)
        emit(s + 1, c)
        return x

    lax.fori_loop(0, (SUBSTEPS - 1) * CHUNKS, step, 0)
    lax.fori_loop(0, CHUNKS, lambda c, x: (assemble(SUBSTEPS - 1, c), x)[1], 0)

    def fall(n, c):
        total = rate[0] * W[n, 0]
        for l in range(1, L):
            total = total + rate[l] * W[n, l]
        RA[n] = total
        return c

    lax.fori_loop(0, N, fall, 0)
    ra2 = split(RA[...].reshape(N * Q, E))

    def gather_node(a):
        where = atmos_node[pl.ds(a, 1), :] // E
        g = fold(dot(ra2, BT[a]))
        total = jnp.where(where == 0, g[:Q], 0.0)
        for n in range(1, N):
            total = total + jnp.where(where == n, g[n * Q : (n + 1) * Q], 0.0)
        out_r[a] = total * w_back[pl.ds(a, 1), :]

    loop(parts, gather_node)

    def copy_r(d, l, p, from_l, from_p):
        return pltpu.make_async_remote_copy(
            src_ref=out_r.at[p],
            dst_ref=in_r.at[from_l, from_p],
            send_sem=r_ss.at[d],
            recv_sem=r_rs.at[from_l, from_p],
            device_id={"sfc": p, "lev": l},
            device_id_type=MESH,
        )

    def start_r(d):
        l, p = peer(d + 1)
        copy_r(d, l, p, lev, sfc).start()

    loop(group - 1, start_r, 8)
    in_r[lev, sfc] = out_r[sfc]

    def put(i, c):
        l, j = i // tiles, lax.rem(i, tiles)
        lane = pl.ds(pl.multiple_of(j * LANES, LANES), LANES)
        for n in range(N):
            TS[j, pl.ds(l * N + n, Q, stride=L * N), :] = W[n, l, :, lane]
        return c

    lax.fori_loop(0, L * tiles, put, 0)
    for j in range(tiles):
        copy_out(j).start()

    def wait_r(d):
        l, p = peer(d + 1)
        copy_r(d, l, p, l, p).wait_recv()

    loop(group - 1, wait_r, 8)
    land[...] = jnp.zeros_like(land)

    def scatter_land(b):
        x = in_r[0, b]
        for l in range(1, levs):
            x = x + in_r[l, b]
        land[...] = land[...] + fold(dot_t(split(x), LT[b]))

    loop(parts, scatter_land)
    land[...] = live * (water[...] + land_step * (land[...] - EV[...]))

    for j in range(tiles):
        copy_out(j).wait()

    def done_e(d):
        p = lax.rem(sfc + d + 1, parts)
        copy_e(p, p, p).wait_send()

    loop(parts - 1, done_e)

    def done_r(d):
        l, p = peer(d + 1)
        copy_r(d, l, p, l, p).wait_send()

    loop(group - 1, done_r, 8)

    def done_halo(i, x):
        for d in range(2):
            halo_copy(i // CHUNKS, lax.rem(i, CHUNKS), d).wait_send()
        return x

    lax.fori_loop(0, SUBSTEPS * CHUNKS, done_halo, 0)


def shards(
    tracers,
    velocity,
    node_mass,
    inverse_mass,
    edge_slots,
    send_rows,
    land_water,
    evap_factor,
    land_counts,
    land_slot,
    atmos_node,
    weight_to_atmos,
    weight_to_land,
    rain_rate,
):
    Q, L, N, E = tracers.shape
    parts = lax.axis_size("sfc")
    levs = lax.axis_size("lev")
    width = send_rows.shape[1]
    land_slots = land_water.shape[1]
    block = land_slot.shape[2]
    R = L // CHUNKS * Q
    vmem = pl.BlockSpec(memory_space=pltpu.VMEM)
    smem = pl.BlockSpec(memory_space=pltpu.SMEM)
    specs = [vmem] * 14
    specs[0] = pl.BlockSpec(memory_space=pl.ANY)
    specs[8] = smem
    specs[13] = smem
    dma = pltpu.SemaphoreType.DMA
    tracers_out, land_out = pl.pallas_call(
        functools.partial(kernel, parts, levs),
        out_shape=(
            jax.ShapeDtypeStruct((Q * L * N, E), F32),
            jax.ShapeDtypeStruct((Q, land_slots), F32),
        ),
        in_specs=specs,
        out_specs=(pl.BlockSpec(memory_space=pl.ANY), vmem),
        scratch_shapes=[
            pltpu.VMEM((E // LANES, Q * L * N, LANES), F32),
            pltpu.VMEM((N, L, Q, E), F32),
            pltpu.VMEM((2, N, L, Q, E), F32),
            pltpu.VMEM((N, Q, E), F32),
            pltpu.VMEM((N, Q, E), F32),
            pltpu.VMEM((N, Q, E), F32),
            pltpu.VMEM((4, E, E), BF16),
            pltpu.VMEM((2, width, E), BF16),
            pltpu.VMEM((2, E, width), BF16),
            pltpu.VMEM((parts, land_slots, block), BF16),
            pltpu.VMEM((parts, E, block), BF16),
            pltpu.VMEM((CHUNKS, 4, 8 * R, E), BF16),
            pltpu.VMEM((4, 4 * R, E), F32),
            pltpu.VMEM((N, Q, E), F32),
            pltpu.VMEM((Q, land_slots), F32),
            pltpu.VMEM((SUBSTEPS, CHUNKS, 2, 4 * R, width), F32),
            pltpu.VMEM((SUBSTEPS, CHUNKS, 2, 4 * R, width), F32),
            pltpu.VMEM((parts, Q, block), F32),
            pltpu.VMEM((parts, Q, block), F32),
            pltpu.VMEM((parts, Q, block), F32),
            pltpu.VMEM((levs, parts, Q, block), F32),
            dma((SUBSTEPS, CHUNKS, 2)),
            dma((SUBSTEPS, CHUNKS, 2)),
            dma((parts,)),
            dma((parts,)),
            dma((parts * levs,)),
            dma((levs, parts)),
            dma((E // LANES,)),
        ],
        compiler_params=pltpu.CompilerParams(
            collective_id=0, has_side_effects=True, vmem_limit_bytes=56 * 1024 * 1024
        ),
    )(
        tracers.reshape(Q * L * N, E),
        velocity.reshape(-1, E),
        node_mass,
        inverse_mass,
        edge_slots,
        send_rows,
        land_water,
        evap_factor.reshape(1, -1),
        land_counts,
        land_slot[0],
        atmos_node[0],
        weight_to_atmos[0],
        weight_to_land[0],
        rain_rate,
    )
    return tracers_out.reshape(Q, L, N, E), land_out


def solution(mesh):
    return jax.shard_map(
        shards,
        mesh=mesh,
        in_specs=(
            P("trc", "lev", None, ("ens", "sfc")),
            P("lev", None, None, ("ens", "sfc")),
            P(None, "sfc"),
            P(None, "sfc"),
            P(None, "sfc"),
            P(None, "sfc"),
            P("trc", ("ens", "sfc")),
            P("sfc"),
            P("sfc"),
            P("sfc", None, None),
            P("sfc", None, None),
            P("sfc", None, None),
            P("sfc", None, None),
            P("lev"),
        ),
        out_specs=(P("trc", "lev", None, ("ens", "sfc")), P("trc", ("ens", "sfc"))),
        check_vma=False,
    )
```

```python
import functools
import math

import jax
import jax.numpy as jnp
import numpy as np
from jax import lax
from jax.experimental import pallas as pl
from jax.experimental.pallas import tpu as pltpu
from jax.sharding import PartitionSpec as P

SUBSTEPS = 4
CHUNKS = 4
LANES = 128
time_step = 0.03
land_step = 0.5
EDGES = ((0, 1, 2, 3), (3, 7, 11, 15), (12, 13, 14, 15), (0, 4, 8, 12))
MESH = pl.DeviceIdType.MESH
F32 = jnp.float32
BF16 = jnp.bfloat16


def derivative_matrix():
    points = [-1.0, -1.0 / math.sqrt(5.0), 1.0 / math.sqrt(5.0), 1.0]
    matrix = np.zeros((4, 4))
    for i in range(4):
        for m in range(4):
            if i != m:
                w_i = np.prod([points[i] - points[o] for o in range(4) if o != i])
                w_m = np.prod([points[m] - points[o] for o in range(4) if o != m])
                matrix[i, m] = w_i / (w_m * (points[i] - points[m]))
        matrix[i, i] = sum(1.0 / (points[i] - points[o]) for o in range(4) if o != i)
    matrix[np.abs(matrix) < 1e-12] = 0.0
    return matrix


def loop(count, body, unroll_to=4):
    if count <= unroll_to:
        for i in range(count):
            body(i)
    else:
        lax.fori_loop(0, count, lambda i, c: (body(i), c)[1], 0)


def split(x):
    high = x.astype(BF16)
    low = (x - high.astype(F32)).astype(BF16)
    return jnp.concatenate([high, low], axis=0)


def fold(y):
    half = y.shape[0] // 2
    return y[:half] + y[half:]


def dot(a, b):
    return jnp.dot(a, b, preferred_element_type=F32)


def dot_t(a, b):
    return lax.dot_general(a, b, (((1,), (1,)), ((), ())), preferred_element_type=F32)


def hot(rows, first, index):
    place = lax.broadcasted_iota(jnp.int32, (rows, index.shape[1]), 0) + first
    return jnp.where(place == index, 1.0, 0.0).astype(BF16)


def kernel(
    parts,
    levs,
    tr,
    vel,
    mass,
    inv,
    slots,
    rows_sent,
    water,
    factor,
    counts,
    land_slot,
    atmos_node,
    w_out,
    w_back,
    rate,
    out,
    land,
    TS,
    W,
    VB,
    MB,
    IB,
    MS,
    OH,
    OHR,
    SOH,
    LT,
    BT,
    HL,
    G,
    RA,
    EV,
    send,
    halo,
    out_e,
    in_e,
    out_r,
    in_r,
    halo_ss,
    halo_rs,
    e_ss,
    e_rs,
    r_ss,
    r_rs,
    t_sem,
    o_sem,
):
    N, L, Q, E = W.shape
    LC = L // CHUNKS
    R = LC * Q
    tiles = E // LANES
    land_slots = water.shape[1]
    sfc = lax.axis_index("sfc")
    lev = lax.axis_index("lev")
    group = parts * levs
    mine = lev * parts + sfc

    def peer(d):
        other = lax.rem(mine + d, group)
        return other // parts, lax.rem(other, parts)

    barrier = pltpu.get_barrier_semaphore()

    def greet(d):
        l, p = peer(d + 1)
        pl.semaphore_signal(barrier, inc=1, device_id={"sfc": p, "lev": l}, device_id_type=MESH)

    loop(group - 1, greet, 8)

    def copy_in(j):
        return pltpu.make_async_copy(
            tr.at[:, pl.ds(j * LANES, LANES)], TS.at[j], t_sem.at[j]
        )

    for j in range(tiles):
        copy_in(j).start()

    def copy_out(c):
        levels = pl.ds(c * LC, LC)
        return pltpu.make_async_copy(W.at[:, levels], out.at[:, levels], o_sem.at[c])

    live = jnp.where(
        lax.broadcasted_iota(jnp.int32, (1, land_slots), 1) < counts[0], 1.0, 0.0
    ).astype(F32)
    w = water[...]
    evaporation = live * factor[...] * w / (1.0 + w)
    EV[...] = evaporation
    ev2 = split(evaporation)

    def gather_land(b):
        LT[b] = hot(land_slots, 0, land_slot[pl.ds(b, 1), :])
        out_e[b] = fold(dot(ev2, LT[b])) * w_out[pl.ds(b, 1), :]

    loop(parts, gather_land)

    def copy_e(src, dst, p):
        return pltpu.make_async_remote_copy(
            src_ref=out_e.at[src],
            dst_ref=in_e.at[dst],
            send_sem=e_ss.at[src],
            recv_sem=e_rs.at[dst],
            device_id={"sfc": p},
            device_id_type=MESH,
        )

    SOH[0] = hot(E, 0, rows_sent[0:1, :])
    SOH[1] = hot(E, 0, rows_sent[1:2, :])
    for n in range(N):
        MB[n] = jnp.broadcast_to(mass[n : n + 1, :], (Q, E))

    def turn(i, c):
        l, j = i // tiles, lax.rem(i, tiles)
        lane = pl.ds(pl.multiple_of(j * LANES, LANES), LANES)
        for n in range(N):
            W[n, l, :, lane] = TS[j, pl.ds(l * N + n, Q, stride=L * N), :]
        for d in range(2):
            v = vel[pl.ds(pl.multiple_of((l * 2 + d) * N, N), N), lane] * time_step
            for n in range(N):
                VB[d, n, l, :, lane] = jnp.broadcast_to(v[n : n + 1], (Q, LANES))
        return c

    for j in range(tiles):
        copy_in(j).wait()
    lax.fori_loop(0, L * tiles, turn, 0)

    D = derivative_matrix()

    def advect(first):
        def one(i, c):
            l, j = first + i // tiles, lax.rem(i, tiles)
            lane = pl.ds(pl.multiple_of(j * LANES, LANES), LANES)
            t = [W[n, l, :, lane] for n in range(N)]
            f = [VB[0, n, l, :, lane] * t[n] for n in range(N)]
            acc = []
            for n in range(N):
                row, i_ = n // 4, n % 4
                terms = [float(D[i_, m]) * f[4 * row + m] for m in range(4) if D[i_, m] != 0.0]
                acc.append(functools.reduce(lambda a, b: a + b, terms))
            f = [VB[1, n, l, :, lane] * t[n] for n in range(N)]
            for n in range(N):
                row, i_ = n // 4, n % 4
                terms = [float(D[row, m]) * f[4 * m + i_] for m in range(4) if D[row, m] != 0.0]
                total = functools.reduce(lambda a, b: a + b, terms)
                W[n, l, :, lane] = MB[n, :, lane] * (t[n] - (acc[n] + total))
            return c

        lax.fori_loop(0, LC * tiles, one, 0)

    def halo_copy(s, c, d):
        other = lax.rem(sfc + (parts - 1 if d == 0 else 1), parts)
        return pltpu.make_async_remote_copy(
            src_ref=send.at[s, c, d],
            dst_ref=halo.at[s, c, d],
            send_sem=halo_ss.at[s, c, d],
            recv_sem=halo_rs.at[s, c, d],
            device_id={"sfc": other},
            device_id_type=MESH,
        )

    def emit(s, c):
        @pl.when(c == CHUNKS - 1)
        def _():
            for n in range(N):
                W[n, L - 1] = W[n, L - 1] + MS[n]

        def edge(k):
            x = jnp.concatenate(
                [W[n, pl.ds(c * LC, LC)].reshape(R, E) for n in EDGES[k]], axis=0
            )
            HL[c, k] = split(x)

        for d in range(2):
            edge(2 * d)
            send[s, c, d] = fold(dot(HL[c, 2 * d], SOH[d]))
            halo_copy(s, c, d).start()
        edge(1)
        edge(3)

    def assemble(s, c):
        for k in range(4):
            G[k] = fold(dot(HL[c, (k + 2) % 4], OH[k]))
        for d in range(2):
            halo_copy(s, c, 1 - d).wait_recv()
            G[2 * d] = G[2 * d] + fold(dot(split(halo[s, c, 1 - d]), OHR[d]))
        for n in range(N):
            x = W[n, pl.ds(c * LC, LC)]
            for k in range(4):
                for t in range(4):
                    if EDGES[k][t] == n:
                        x = x + G[k, t * R : (t + 1) * R].reshape(LC, Q, E)
            W[n, pl.ds(c * LC, LC)] = x * IB[n][None]

    pl.semaphore_wait(barrier, group - 1)
    def start_e(d):
        p = lax.rem(sfc + d + 1, parts)
        copy_e(p, sfc, p).start()

    loop(parts - 1, start_e)
    in_e[sfc] = out_e[sfc]

    def first(c, x):
        advect(c * LC)
        emit(0, c)
        return x

    lax.fori_loop(0, CHUNKS - 1, first, 0)
    def build_slots(i):
        k, r = i // tiles, lax.rem(i, tiles)
        first = r * LANES
        OH[k, pl.ds(pl.multiple_of(first, LANES), LANES), :] = hot(
            LANES, first, slots[pl.ds(k, 1), :]
        )

    lax.fori_loop(0, 4 * tiles, lambda i, c: (build_slots(i), c)[1], 0)
    width = rows_sent.shape[1]
    OHR[0] = hot(width, E, slots[0:1, :])
    OHR[1] = hot(width, E + width, slots[2:3, :])

    def build_node(b):
        node = atmos_node[pl.ds(b, 1), :]
        BT[b] = hot(E, 0, lax.rem(node, E))

    loop(parts, build_node)
    for n in range(N):
        IB[n] = jnp.broadcast_to(inv[n : n + 1, :], (Q, E))
    advect((CHUNKS - 1) * LC)

    def wait_e(d):
        p = lax.rem(sfc + d + 1, parts)
        copy_e(p, p, p).wait_recv()

    loop(parts - 1, wait_e)
    MS[...] = jnp.zeros_like(MS)

    def scatter_node(a):
        where = atmos_node[pl.ds(a, 1), :] // E
        x = in_e[a]
        x = jnp.concatenate([jnp.where(where == n, x, 0.0) for n in range(N)], axis=0)
        MS[...] = MS[...] + fold(dot_t(split(x), BT[a])).reshape(N, Q, E)

    loop(parts, scatter_node)
    bottom = jnp.where(lev == levs - 1, time_step, 0.0).astype(F32)
    MS[...] = MS[...] * MB[...] * bottom
    emit(0, CHUNKS - 1)

    def step(i, x):
        s, c = i // CHUNKS, lax.rem(i, CHUNKS)
        assemble(s, c)
        advect(c * LC)
        emit(s + 1, c)
        return x

    lax.fori_loop(0, (SUBSTEPS - 1) * CHUNKS, step, 0)

    def last(c, x):
        assemble(SUBSTEPS - 1, c)
        copy_out(c).start()
        return x

    lax.fori_loop(0, CHUNKS, last, 0)

    def fall(n, c):
        total = rate[0] * W[n, 0]
        for l in range(1, L):
            total = total + rate[l] * W[n, l]
        RA[n] = total
        return c

    lax.fori_loop(0, N, fall, 0)
    ra2 = split(RA[...].reshape(N * Q, E))

    def gather_node(a):
        where = atmos_node[pl.ds(a, 1), :] // E
        g = fold(dot(ra2, BT[a]))
        total = jnp.where(where == 0, g[:Q], 0.0)
        for n in range(1, N):
            total = total + jnp.where(where == n, g[n * Q : (n + 1) * Q], 0.0)
        out_r[a] = total * w_back[pl.ds(a, 1), :]

    loop(parts, gather_node)

    def copy_r(d, l, p, from_l, from_p):
        return pltpu.make_async_remote_copy(
            src_ref=out_r.at[p],
            dst_ref=in_r.at[from_l, from_p],
            send_sem=r_ss.at[d],
            recv_sem=r_rs.at[from_l, from_p],
            device_id={"sfc": p, "lev": l},
            device_id_type=MESH,
        )

    def start_r(d):
        l, p = peer(d + 1)
        copy_r(d, l, p, lev, sfc).start()

    loop(group - 1, start_r, 8)
    in_r[lev, sfc] = out_r[sfc]

    def wait_r(d):
        l, p = peer(d + 1)
        copy_r(d, l, p, l, p).wait_recv()

    loop(group - 1, wait_r, 8)
    land[...] = jnp.zeros_like(land)

    def scatter_land(b):
        x = in_r[0, b]
        for l in range(1, levs):
            x = x + in_r[l, b]
        land[...] = land[...] + fold(dot_t(split(x), LT[b]))

    loop(parts, scatter_land)
    land[...] = live * (water[...] + land_step * (land[...] - EV[...]))

    for c in range(CHUNKS):
        copy_out(c).wait()

    def done_e(d):
        p = lax.rem(sfc + d + 1, parts)
        copy_e(p, p, p).wait_send()

    loop(parts - 1, done_e)

    def done_r(d):
        l, p = peer(d + 1)
        copy_r(d, l, p, l, p).wait_send()

    loop(group - 1, done_r, 8)

    def done_halo(i, x):
        for d in range(2):
            halo_copy(i // CHUNKS, lax.rem(i, CHUNKS), d).wait_send()
        return x

    lax.fori_loop(0, SUBSTEPS * CHUNKS, done_halo, 0)


def finish(w, land_in, out, land, turned):
    N, pair, Q, E = w.shape
    for l in range(pair):
        for j in range(E // LANES):
            lane = slice(j * LANES, (j + 1) * LANES)
            for n in range(N):
                turned[l, j, pl.ds(n, Q, stride=N), :] = w[n, l, :, lane]
            for q in range(Q):
                out[q, l, :, lane] = turned[l, j, q * N : (q + 1) * N, :]
    land[...] = land_in[...]


def shards(
    tracers,
    velocity,
    node_mass,
    inverse_mass,
    edge_slots,
    send_rows,
    land_water,
    evap_factor,
    land_counts,
    land_slot,
    atmos_node,
    weight_to_atmos,
    weight_to_land,
    rain_rate,
):
    Q, L, N, E = tracers.shape
    parts = lax.axis_size("sfc")
    levs = lax.axis_size("lev")
    width = send_rows.shape[1]
    land_slots = land_water.shape[1]
    block = land_slot.shape[2]
    R = L // CHUNKS * Q
    vmem = pl.BlockSpec(memory_space=pltpu.VMEM)
    smem = pl.BlockSpec(memory_space=pltpu.SMEM)
    specs = [vmem] * 14
    specs[0] = pl.BlockSpec(memory_space=pl.ANY)
    specs[8] = smem
    specs[13] = smem
    dma = pltpu.SemaphoreType.DMA
    nodes_first, land_sum = pl.pallas_call(
        functools.partial(kernel, parts, levs),
        out_shape=(
            jax.ShapeDtypeStruct((N, L, Q, E), F32),
            jax.ShapeDtypeStruct((Q, land_slots), F32),
        ),
        in_specs=specs,
        out_specs=(pl.BlockSpec(memory_space=pl.ANY), vmem),
        scratch_shapes=[
            pltpu.VMEM((E // LANES, Q * L * N, LANES), F32),
            pltpu.VMEM((N, L, Q, E), F32),
            pltpu.VMEM((2, N, L, Q, E), F32),
            pltpu.VMEM((N, Q, E), F32),
            pltpu.VMEM((N, Q, E), F32),
            pltpu.VMEM((N, Q, E), F32),
            pltpu.VMEM((4, E, E), BF16),
            pltpu.VMEM((2, width, E), BF16),
            pltpu.VMEM((2, E, width), BF16),
            pltpu.VMEM((parts, land_slots, block), BF16),
            pltpu.VMEM((parts, E, block), BF16),
            pltpu.VMEM((CHUNKS, 4, 8 * R, E), BF16),
            pltpu.VMEM((4, 4 * R, E), F32),
            pltpu.VMEM((N, Q, E), F32),
            pltpu.VMEM((Q, land_slots), F32),
            pltpu.VMEM((SUBSTEPS, CHUNKS, 2, 4 * R, width), F32),
            pltpu.VMEM((SUBSTEPS, CHUNKS, 2, 4 * R, width), F32),
            pltpu.VMEM((parts, Q, block), F32),
            pltpu.VMEM((parts, Q, block), F32),
            pltpu.VMEM((parts, Q, block), F32),
            pltpu.VMEM((levs, parts, Q, block), F32),
            dma((SUBSTEPS, CHUNKS, 2)),
            dma((SUBSTEPS, CHUNKS, 2)),
            dma((parts,)),
            dma((parts,)),
            dma((parts * levs,)),
            dma((levs, parts)),
            dma((E // LANES,)),
            dma((CHUNKS,)),
        ],
        compiler_params=pltpu.CompilerParams(
            collective_id=0, has_side_effects=True, vmem_limit_bytes=56 * 1024 * 1024
        ),
    )(
        tracers.reshape(Q * L * N, E),
        velocity.reshape(-1, E),
        node_mass,
        inverse_mass,
        edge_slots,
        send_rows,
        land_water,
        evap_factor.reshape(1, -1),
        land_counts,
        land_slot[0],
        atmos_node[0],
        weight_to_atmos[0],
        weight_to_land[0],
        rain_rate,
    )
    pair = math.gcd(L, 4)
    return pl.pallas_call(
        finish,
        grid=(L // pair,),
        out_shape=(
            jax.ShapeDtypeStruct((Q, L, N, E), F32),
            jax.ShapeDtypeStruct((Q, land_slots), F32),
        ),
        in_specs=[
            pl.BlockSpec((N, pair, Q, E), lambda i: (0, i, 0, 0)),
            pl.BlockSpec((Q, land_slots), lambda i: (0, 0)),
        ],
        out_specs=(
            pl.BlockSpec((Q, pair, N, E), lambda i: (0, i, 0, 0)),
            pl.BlockSpec((Q, land_slots), lambda i: (0, 0)),
        ),
        scratch_shapes=[pltpu.VMEM((pair, E // LANES, Q * N, LANES), F32)],
    )(nodes_first, land_sum)


def solution(mesh):
    return jax.shard_map(
        shards,
        mesh=mesh,
        in_specs=(
            P("trc", "lev", None, ("ens", "sfc")),
            P("lev", None, None, ("ens", "sfc")),
            P(None, "sfc"),
            P(None, "sfc"),
            P(None, "sfc"),
            P(None, "sfc"),
            P("trc", ("ens", "sfc")),
            P("sfc"),
            P("sfc"),
            P("sfc", None, None),
            P("sfc", None, None),
            P("sfc", None, None),
            P("sfc", None, None),
            P("lev"),
        ),
        out_specs=(P("trc", "lev", None, ("ens", "sfc")), P("trc", ("ens", "sfc"))),
        check_vma=False,
    )
```

```python
import functools
import math

import jax
import jax.numpy as jnp
import numpy as np
from jax import lax
from jax.experimental import pallas as pl
from jax.experimental.pallas import tpu as pltpu
from jax.sharding import PartitionSpec as P

SUBSTEPS = 4
CHUNKS = 4
LANES = 128
time_step = 0.03
land_step = 0.5
EDGES = ((0, 1, 2, 3), (3, 7, 11, 15), (12, 13, 14, 15), (0, 4, 8, 12))
MESH = pl.DeviceIdType.MESH
F32 = jnp.float32
BF16 = jnp.bfloat16


def derivative_matrix():
    points = [-1.0, -1.0 / math.sqrt(5.0), 1.0 / math.sqrt(5.0), 1.0]
    matrix = np.zeros((4, 4))
    for i in range(4):
        for m in range(4):
            if i != m:
                w_i = np.prod([points[i] - points[o] for o in range(4) if o != i])
                w_m = np.prod([points[m] - points[o] for o in range(4) if o != m])
                matrix[i, m] = w_i / (w_m * (points[i] - points[m]))
        matrix[i, i] = sum(1.0 / (points[i] - points[o]) for o in range(4) if o != i)
    matrix[np.abs(matrix) < 1e-12] = 0.0
    return matrix


def loop(count, body, unroll_to=4):
    if count <= unroll_to:
        for i in range(count):
            body(i)
    else:
        lax.fori_loop(0, count, lambda i, c: (body(i), c)[1], 0)


def split(x):
    high = x.astype(BF16)
    low = (x - high.astype(F32)).astype(BF16)
    return jnp.concatenate([high, low], axis=0)


def fold(y):
    half = y.shape[0] // 2
    return y[:half] + y[half:]


def dot(a, b):
    return jnp.dot(a, b, preferred_element_type=F32)


def dot_t(a, b):
    return lax.dot_general(a, b, (((1,), (1,)), ((), ())), preferred_element_type=F32)


def hot(rows, first, index):
    place = lax.broadcasted_iota(jnp.int32, (rows, index.shape[1]), 0) + first
    return jnp.where(place == index, 1.0, 0.0).astype(BF16)


def kernel(
    parts,
    levs,
    tr,
    vel,
    mass,
    inv,
    slots,
    rows_sent,
    water,
    factor,
    counts,
    land_slot,
    atmos_node,
    w_out,
    w_back,
    rate,
    out,
    land,
    TS,
    W,
    VB,
    MB,
    IB,
    MS,
    OH,
    OHR,
    SOH,
    LT,
    BT,
    HL,
    G,
    RA,
    EV,
    send,
    halo,
    out_e,
    in_e,
    out_r,
    in_r,
    halo_ss,
    halo_rs,
    e_ss,
    e_rs,
    r_ss,
    r_rs,
    t_sem,
    o_sem,
):
    N, L, Q, E = W.shape
    LC = L // CHUNKS
    R = LC * Q
    tiles = E // LANES
    land_slots = water.shape[1]
    sfc = lax.axis_index("sfc")
    lev = lax.axis_index("lev")
    group = parts * levs
    mine = lev * parts + sfc

    def peer(d):
        other = lax.rem(mine + d, group)
        return other // parts, lax.rem(other, parts)

    barrier = pltpu.get_barrier_semaphore()

    def greet(d):
        l, p = peer(d + 1)
        pl.semaphore_signal(barrier, inc=1, device_id={"sfc": p, "lev": l}, device_id_type=MESH)

    loop(group - 1, greet, 8)

    def copy_in(j):
        return pltpu.make_async_copy(
            tr.at[:, pl.ds(j * LANES, LANES)], TS.at[j], t_sem.at[j]
        )

    for j in range(tiles):
        copy_in(j).start()

    def copy_out(c):
        levels = pl.ds(c * LC, LC)
        return pltpu.make_async_copy(W.at[:, levels], out.at[:, levels], o_sem.at[c])

    live = jnp.where(
        lax.broadcasted_iota(jnp.int32, (1, land_slots), 1) < counts[0], 1.0, 0.0
    ).astype(F32)
    w = water[...]
    evaporation = live * factor[...] * w / (1.0 + w)
    EV[...] = evaporation
    ev2 = split(evaporation)

    def gather_land(b):
        LT[b] = hot(land_slots, 0, land_slot[pl.ds(b, 1), :])
        out_e[b] = fold(dot(ev2, LT[b])) * w_out[pl.ds(b, 1), :]

    loop(parts, gather_land)

    def copy_e(src, dst, p):
        return pltpu.make_async_remote_copy(
            src_ref=out_e.at[src],
            dst_ref=in_e.at[dst],
            send_sem=e_ss.at[src],
            recv_sem=e_rs.at[dst],
            device_id={"sfc": p},
            device_id_type=MESH,
        )

    SOH[0] = hot(E, 0, rows_sent[0:1, :])
    SOH[1] = hot(E, 0, rows_sent[1:2, :])
    for n in range(N):
        MB[n] = jnp.broadcast_to(mass[n : n + 1, :], (Q, E))

    def turn(i, c):
        l, j = i // tiles, lax.rem(i, tiles)
        lane = pl.ds(pl.multiple_of(j * LANES, LANES), LANES)
        for n in range(N):
            W[n, l, :, lane] = TS[j, pl.ds(l * N + n, Q, stride=L * N), :]
        for d in range(2):
            v = vel[pl.ds(pl.multiple_of((l * 2 + d) * N, N), N), lane] * time_step
            for n in range(N):
                VB[d, n, l, :, lane] = jnp.broadcast_to(v[n : n + 1], (Q, LANES))
        return c

    for j in range(tiles):
        copy_in(j).wait()
    lax.fori_loop(0, L * tiles, turn, 0)

    D = derivative_matrix()

    def advect(first):
        def one(i, c):
            l, j = first + i // tiles, lax.rem(i, tiles)
            lane = pl.ds(pl.multiple_of(j * LANES, LANES), LANES)
            t = [W[n, l, :, lane] for n in range(N)]
            f = [VB[0, n, l, :, lane] * t[n] for n in range(N)]
            acc = []
            for n in range(N):
                row, i_ = n // 4, n % 4
                terms = [float(D[i_, m]) * f[4 * row + m] for m in range(4) if D[i_, m] != 0.0]
                acc.append(functools.reduce(lambda a, b: a + b, terms))
            f = [VB[1, n, l, :, lane] * t[n] for n in range(N)]
            for n in range(N):
                row, i_ = n // 4, n % 4
                terms = [float(D[row, m]) * f[4 * m + i_] for m in range(4) if D[row, m] != 0.0]
                total = functools.reduce(lambda a, b: a + b, terms)
                W[n, l, :, lane] = MB[n, :, lane] * (t[n] - (acc[n] + total))
            return c

        lax.fori_loop(0, LC * tiles, one, 0, unroll=2)

    def halo_copy(s, c, d):
        other = lax.rem(sfc + (parts - 1 if d == 0 else 1), parts)
        return pltpu.make_async_remote_copy(
            src_ref=send.at[s, c, d],
            dst_ref=halo.at[s, c, d],
            send_sem=halo_ss.at[s, c, d],
            recv_sem=halo_rs.at[s, c, d],
            device_id={"sfc": other},
            device_id_type=MESH,
        )

    def emit(s, c):
        @pl.when(c == CHUNKS - 1)
        def _():
            for n in range(N):
                W[n, L - 1] = W[n, L - 1] + MS[n]

        def edge(k):
            x = jnp.concatenate(
                [W[n, pl.ds(c * LC, LC)].reshape(R, E) for n in EDGES[k]], axis=0
            )
            HL[c, k] = split(x)

        for d in range(2):
            edge(2 * d)
            send[s, c, d] = fold(dot(HL[c, 2 * d], SOH[d]))
            halo_copy(s, c, d).start()
        edge(1)
        edge(3)

    def assemble(s, c):
        for k in range(4):
            G[k] = fold(dot(HL[c, (k + 2) % 4], OH[k]))
        for d in range(2):
            halo_copy(s, c, 1 - d).wait_recv()
            G[2 * d] = G[2 * d] + fold(dot(split(halo[s, c, 1 - d]), OHR[d]))
        for n in range(N):
            x = W[n, pl.ds(c * LC, LC)]
            for k in range(4):
                for t in range(4):
                    if EDGES[k][t] == n:
                        x = x + G[k, t * R : (t + 1) * R].reshape(LC, Q, E)
            W[n, pl.ds(c * LC, LC)] = x * IB[n][None]

    pl.semaphore_wait(barrier, group - 1)
    def start_e(d):
        p = lax.rem(sfc + d + 1, parts)
        copy_e(p, sfc, p).start()

    loop(parts - 1, start_e)
    in_e[sfc] = out_e[sfc]

    def first(c, x):
        advect(c * LC)
        emit(0, c)
        return x

    lax.fori_loop(0, CHUNKS - 1, first, 0)
    def build_slots(i):
        k, r = i // tiles, lax.rem(i, tiles)
        first = r * LANES
        OH[k, pl.ds(pl.multiple_of(first, LANES), LANES), :] = hot(
            LANES, first, slots[pl.ds(k, 1), :]
        )

    lax.fori_loop(0, 4 * tiles, lambda i, c: (build_slots(i), c)[1], 0)
    width = rows_sent.shape[1]
    OHR[0] = hot(width, E, slots[0:1, :])
    OHR[1] = hot(width, E + width, slots[2:3, :])

    def build_node(b):
        node = atmos_node[pl.ds(b, 1), :]
        BT[b] = hot(E, 0, lax.rem(node, E))

    loop(parts, build_node)
    for n in range(N):
        IB[n] = jnp.broadcast_to(inv[n : n + 1, :], (Q, E))
    advect((CHUNKS - 1) * LC)

    def wait_e(d):
        p = lax.rem(sfc + d + 1, parts)
        copy_e(p, p, p).wait_recv()

    loop(parts - 1, wait_e)
    MS[...] = jnp.zeros_like(MS)

    def scatter_node(a):
        where = atmos_node[pl.ds(a, 1), :] // E
        x = in_e[a]
        x = jnp.concatenate([jnp.where(where == n, x, 0.0) for n in range(N)], axis=0)
        MS[...] = MS[...] + fold(dot_t(split(x), BT[a])).reshape(N, Q, E)

    loop(parts, scatter_node)
    bottom = jnp.where(lev == levs - 1, time_step, 0.0).astype(F32)
    MS[...] = MS[...] * MB[...] * bottom
    emit(0, CHUNKS - 1)

    def step(i, x):
        s, c = i // CHUNKS, lax.rem(i, CHUNKS)
        assemble(s, c)
        advect(c * LC)
        emit(s + 1, c)
        return x

    lax.fori_loop(0, (SUBSTEPS - 1) * CHUNKS, step, 0)

    def last(c, x):
        assemble(SUBSTEPS - 1, c)
        copy_out(c).start()
        return x

    lax.fori_loop(0, CHUNKS, last, 0)

    def fall(n, c):
        total = rate[0] * W[n, 0]
        for l in range(1, L):
            total = total + rate[l] * W[n, l]
        RA[n] = total
        return c

    lax.fori_loop(0, N, fall, 0)
    ra2 = split(RA[...].reshape(N * Q, E))

    def gather_node(a):
        where = atmos_node[pl.ds(a, 1), :] // E
        g = fold(dot(ra2, BT[a]))
        total = jnp.where(where == 0, g[:Q], 0.0)
        for n in range(1, N):
            total = total + jnp.where(where == n, g[n * Q : (n + 1) * Q], 0.0)
        out_r[a] = total * w_back[pl.ds(a, 1), :]

    loop(parts, gather_node)

    def copy_r(d, l, p, from_l, from_p):
        return pltpu.make_async_remote_copy(
            src_ref=out_r.at[p],
            dst_ref=in_r.at[from_l, from_p],
            send_sem=r_ss.at[d],
            recv_sem=r_rs.at[from_l, from_p],
            device_id={"sfc": p, "lev": l},
            device_id_type=MESH,
        )

    def start_r(d):
        l, p = peer(d + 1)
        copy_r(d, l, p, lev, sfc).start()

    loop(group - 1, start_r, 8)
    in_r[lev, sfc] = out_r[sfc]

    def wait_r(d):
        l, p = peer(d + 1)
        copy_r(d, l, p, l, p).wait_recv()

    loop(group - 1, wait_r, 8)
    land[...] = jnp.zeros_like(land)

    def scatter_land(b):
        x = in_r[0, b]
        for l in range(1, levs):
            x = x + in_r[l, b]
        land[...] = land[...] + fold(dot_t(split(x), LT[b]))

    loop(parts, scatter_land)
    land[...] = live * (water[...] + land_step * (land[...] - EV[...]))

    for c in range(CHUNKS):
        copy_out(c).wait()

    def done_e(d):
        p = lax.rem(sfc + d + 1, parts)
        copy_e(p, p, p).wait_send()

    loop(parts - 1, done_e)

    def done_r(d):
        l, p = peer(d + 1)
        copy_r(d, l, p, l, p).wait_send()

    loop(group - 1, done_r, 8)

    def done_halo(i, x):
        for d in range(2):
            halo_copy(i // CHUNKS, lax.rem(i, CHUNKS), d).wait_send()
        return x

    lax.fori_loop(0, SUBSTEPS * CHUNKS, done_halo, 0)


def finish(w, land_in, out, land, turned):
    N, pair, Q, E = w.shape
    for l in range(pair):
        for j in range(E // LANES):
            lane = slice(j * LANES, (j + 1) * LANES)
            for n in range(N):
                turned[l, j, pl.ds(n, Q, stride=N), :] = w[n, l, :, lane]
            for q in range(Q):
                out[q, l, :, lane] = turned[l, j, q * N : (q + 1) * N, :]
    land[...] = land_in[...]


def shards(
    tracers,
    velocity,
    node_mass,
    inverse_mass,
    edge_slots,
    send_rows,
    land_water,
    evap_factor,
    land_counts,
    land_slot,
    atmos_node,
    weight_to_atmos,
    weight_to_land,
    rain_rate,
):
    Q, L, N, E = tracers.shape
    parts = lax.axis_size("sfc")
    levs = lax.axis_size("lev")
    width = send_rows.shape[1]
    land_slots = land_water.shape[1]
    block = land_slot.shape[2]
    R = L // CHUNKS * Q
    vmem = pl.BlockSpec(memory_space=pltpu.VMEM)
    smem = pl.BlockSpec(memory_space=pltpu.SMEM)
    specs = [vmem] * 14
    specs[0] = pl.BlockSpec(memory_space=pl.ANY)
    specs[8] = smem
    specs[13] = smem
    dma = pltpu.SemaphoreType.DMA
    nodes_first, land_sum = pl.pallas_call(
        functools.partial(kernel, parts, levs),
        out_shape=(
            jax.ShapeDtypeStruct((N, L, Q, E), F32),
            jax.ShapeDtypeStruct((Q, land_slots), F32),
        ),
        in_specs=specs,
        out_specs=(pl.BlockSpec(memory_space=pl.ANY), vmem),
        scratch_shapes=[
            pltpu.VMEM((E // LANES, Q * L * N, LANES), F32),
            pltpu.VMEM((N, L, Q, E), F32),
            pltpu.VMEM((2, N, L, Q, E), F32),
            pltpu.VMEM((N, Q, E), F32),
            pltpu.VMEM((N, Q, E), F32),
            pltpu.VMEM((N, Q, E), F32),
            pltpu.VMEM((4, E, E), BF16),
            pltpu.VMEM((2, width, E), BF16),
            pltpu.VMEM((2, E, width), BF16),
            pltpu.VMEM((parts, land_slots, block), BF16),
            pltpu.VMEM((parts, E, block), BF16),
            pltpu.VMEM((CHUNKS, 4, 8 * R, E), BF16),
            pltpu.VMEM((4, 4 * R, E), F32),
            pltpu.VMEM((N, Q, E), F32),
            pltpu.VMEM((Q, land_slots), F32),
            pltpu.VMEM((SUBSTEPS, CHUNKS, 2, 4 * R, width), F32),
            pltpu.VMEM((SUBSTEPS, CHUNKS, 2, 4 * R, width), F32),
            pltpu.VMEM((parts, Q, block), F32),
            pltpu.VMEM((parts, Q, block), F32),
            pltpu.VMEM((parts, Q, block), F32),
            pltpu.VMEM((levs, parts, Q, block), F32),
            dma((SUBSTEPS, CHUNKS, 2)),
            dma((SUBSTEPS, CHUNKS, 2)),
            dma((parts,)),
            dma((parts,)),
            dma((parts * levs,)),
            dma((levs, parts)),
            dma((E // LANES,)),
            dma((CHUNKS,)),
        ],
        compiler_params=pltpu.CompilerParams(
            collective_id=0, has_side_effects=True, vmem_limit_bytes=56 * 1024 * 1024
        ),
    )(
        tracers.reshape(Q * L * N, E),
        velocity.reshape(-1, E),
        node_mass,
        inverse_mass,
        edge_slots,
        send_rows,
        land_water,
        evap_factor.reshape(1, -1),
        land_counts,
        land_slot[0],
        atmos_node[0],
        weight_to_atmos[0],
        weight_to_land[0],
        rain_rate,
    )
    pair = math.gcd(L, 4)
    return pl.pallas_call(
        finish,
        grid=(L // pair,),
        out_shape=(
            jax.ShapeDtypeStruct((Q, L, N, E), F32),
            jax.ShapeDtypeStruct((Q, land_slots), F32),
        ),
        in_specs=[
            pl.BlockSpec((N, pair, Q, E), lambda i: (0, i, 0, 0)),
            pl.BlockSpec((Q, land_slots), lambda i: (0, 0)),
        ],
        out_specs=(
            pl.BlockSpec((Q, pair, N, E), lambda i: (0, i, 0, 0)),
            pl.BlockSpec((Q, land_slots), lambda i: (0, 0)),
        ),
        scratch_shapes=[pltpu.VMEM((pair, E // LANES, Q * N, LANES), F32)],
    )(nodes_first, land_sum)


def solution(mesh):
    return jax.shard_map(
        shards,
        mesh=mesh,
        in_specs=(
            P("trc", "lev", None, ("ens", "sfc")),
            P("lev", None, None, ("ens", "sfc")),
            P(None, "sfc"),
            P(None, "sfc"),
            P(None, "sfc"),
            P(None, "sfc"),
            P("trc", ("ens", "sfc")),
            P("sfc"),
            P("sfc"),
            P("sfc", None, None),
            P("sfc", None, None),
            P("sfc", None, None),
            P("sfc", None, None),
            P("lev"),
        ),
        out_specs=(P("trc", "lev", None, ("ens", "sfc")), P("trc", ("ens", "sfc"))),
        check_vma=False,
    )
```
